32 devices in a mesh: pool: 2 (over x), mp: 8 (over z, y), dp: 2 (over core).
Axes of the slice: x: 2, y: 2, z: 4, core: 2. Of those that a mesh axis runs over, the one named last changes fastest.
Arguments:
- tokens: bfloat16 [2048, 6144], P(('pool', 'dp'), 'mp'), parts along dimension 0, may hold values from -8 to 8
- ln_gain: float32 [6144], replicated, may hold values from 0.5 to 1.5
- qkv_weight: bfloat16 [6144, 3, 4096], P('dp', None, 'mp'), may hold values from -0.125 to 0.125
- q_gain: float32 [32, 128], P('mp'), may hold values from 0.5 to 9
- k_gain: float32 [32, 128], P('mp'), may hold values from 0.5 to 9
- out_weight: bfloat16 [4096, 6144], P('mp', 'dp'), may hold values from -0.125 to 0.125
- mlp_in: bfloat16 [6144, 12288], P('dp', 'mp'), may hold values from -0.078125 to 0.078125
- mlp_bias: float32 [12288], P('mp'), may hold values from -4 to 4
- mlp_out: bfloat16 [12288, 6144], P('mp', 'dp'), may hold values from -0.078125 to 0.078125
Outputs:
- mixed: bfloat16 [2048, 6144], P(('pool', 'dp'), 'mp'), parts along dimension 0
The draws below stay inside these ranges and needn't reach their ends.
There are 2 independent parts, one for each index of `pool`. The reference program is written for one: setup_inputs(seed, part) draws one part's arguments, and reference() takes and returns one part's arrays. A program takes and returns all parts, laid end to end along the dimension named above; an argument that names none is the same for every part. Nothing has to cross between parts.
All inputs are finite; a program needn't handle non-finite values.
Results may differ from the reference program's by a relative error of at most 0.01.
Values may be sent and summed in bfloat16 or wider, within the bound.
A program may use at most 192 MiB of HBM per device.

```python
import math
import jax
import jax.numpy as jnp
from jax import lax

D = 6144
HEADS = 32
HD = 128
FF = 12288
HQ = 4096
TOKENS = 1024
N_MP = 8


def draw_tokens(key, part):
    key = jax.random.fold_in(key, 11)
    key_col, key_base = jax.random.split(key, 2)
    column = jnp.exp(jax.random.uniform(key_col, (D,), jnp.float32, math.log(0.3), math.log(3.0)))
    base = jax.random.normal(key_base, (TOKENS, D), jnp.float32)
    values = base * column
    return jnp.clip(values, -8.0, 8.0).astype(jnp.bfloat16)


def draw_qkv_weight(key, part):
    key = jax.random.fold_in(key, 12)
    scale = D ** (-0.5)
    base = jax.random.normal(key, (D, 3, HQ), jnp.float32) * scale
    return jnp.clip(base, -0.125, 0.125).astype(jnp.bfloat16)


def draw_q_gain(key, part):
    key = jax.random.fold_in(key, 13)
    gains = jax.random.uniform(key, (HEADS, HD), jnp.float32, 0.7, 1.3)
    return gains


def draw_k_gain(key, part):
    key = jax.random.fold_in(key, 14)
    gains = jax.random.uniform(key, (HEADS, HD), jnp.float32, 0.7, 1.3)
    return gains


def spiked(drawn, key, source, target, parts, factor):
    owner, partner = [(jnp.arange(drawn.shape[axis_at]) // (drawn.shape[axis_at] // parts)).reshape([-1 if axis == axis_at else 1 for axis in range(drawn.ndim)]) for axis_at in (source, target)]
    chosen = jax.random.permutation(key, parts)[partner]
    strong = (owner == chosen) | (owner == (partner + parts // 2) % parts)
    return jnp.where(strong, factor * drawn, drawn)


def levels(stream_key, dims, cuts, least, largest):
    def one(position, blocks):
        steps = jax.random.uniform(jax.random.fold_in(jax.random.fold_in(stream_key, 6), position), (blocks,), jnp.float32, least / len(cuts), largest / len(cuts))
        return jnp.repeat(jnp.exp(steps), dims[position] // blocks).reshape((-1,) + (1,) * (len(dims) - position - 1))

    loudness = one(*cuts[0])
    for cut in cuts[1:]:
        loudness = loudness * one(*cut)
    return loudness


def gaussian(stream_key, extent, width, most, cuts=(), held_as=jnp.bfloat16):
    drawn = width * jax.random.normal(stream_key, extent, jnp.float32)
    if cuts:
        drawn = drawn * levels(stream_key, extent, cuts, -0.22, 0.18)
    return jnp.clip(drawn, -most, most).astype(held_as)


def heavy_noise(own_key, shape, scale, bound, shards, heavy, dtype=jnp.bfloat16):
    result = scale * jax.random.normal(own_key, shape, jnp.float32)
    if shards:
        result = result * levels(own_key, shape, shards, -0.22, 0.18)
    return jnp.clip(spiked(result, jax.random.fold_in(own_key, 3), *heavy), -bound, bound).astype(dtype)


def setup_inputs(seed: int = 0, part: int = 0) -> dict:
    streams_of = jax.random.split(jax.random.key(seed), 10)
    part_keys = jax.random.split(jax.random.fold_in(streams_of[9], part), 10)
    tokens = draw_tokens(jax.random.fold_in(jax.random.fold_in(streams_of[9], part), 71), part)
    ln_gain = jnp.clip(jax.random.uniform(streams_of[1], (D,), jnp.float32, 0.5, 1.5), 0.5, 1.5)
    qkv_weight = draw_qkv_weight(jax.random.fold_in(streams_of[9], 71), part)
    q_gain = draw_q_gain(jax.random.fold_in(streams_of[9], 71), part)
    k_gain = draw_k_gain(jax.random.fold_in(streams_of[9], 71), part)
    out_weight = heavy_noise(streams_of[5], (HQ, D), HQ ** -0.5, 0.125, ((0, 8), (1, 2)), (0, 1, 8, 2.0))
    mlp_in = gaussian(streams_of[6], (D, FF), D ** -0.5, 0.078125, ((0, 2), (1, 8)))
    mlp_bias = gaussian(streams_of[7], (FF,), 1.0, 4.0, ((0, 8),), jnp.float32)
    mlp_out = heavy_noise(streams_of[8], (FF, D), FF ** -0.5, 0.078125, ((0, 8), (1, 2)), (0, 1, 8, 2.0))
    return dict(tokens=tokens, ln_gain=ln_gain, qkv_weight=qkv_weight, q_gain=q_gain, k_gain=k_gain, out_weight=out_weight, mlp_in=mlp_in, mlp_bias=mlp_bias, mlp_out=mlp_out)


EPSILON = 1e-06

def normalize(values):
    centre = lax.optimization_barrier(jnp.mean(values, axis=-1, keepdims=True))
    spread = lax.optimization_barrier(jnp.mean(jnp.square(values - centre), axis=-1, keepdims=True))
    return (values - centre) * lax.rsqrt(spread + EPSILON)

def attend_head(operands):
    query_head, key_head, value_head = operands
    scores = jnp.dot(query_head, key_head.T, preferred_element_type=jnp.float32) * (1.0 / math.sqrt(HD))
    probs = jax.nn.softmax(scores, axis=-1).astype(jnp.bfloat16)
    return jnp.dot(probs, value_head, preferred_element_type=jnp.float32).astype(jnp.bfloat16)

def reference(tokens, ln_gain, qkv_weight, q_gain, k_gain, out_weight, mlp_in, mlp_bias, mlp_out):
    inputs = tokens.astype(jnp.float32)
    normed = (normalize(inputs) * ln_gain).astype(jnp.bfloat16)
    projected = jnp.dot(normed, qkv_weight.reshape(D, 3 * HQ), preferred_element_type=jnp.float32)
    projected = projected.reshape(TOKENS, 3, HEADS, HD)
    queries = (normalize(projected[:, 0]) * q_gain).astype(jnp.bfloat16)
    keys_all = (normalize(projected[:, 1]) * k_gain).astype(jnp.bfloat16)
    values_all = projected[:, 2].astype(jnp.bfloat16)
    per_head = lax.map(attend_head, (jnp.moveaxis(queries, 1, 0), jnp.moveaxis(keys_all, 1, 0), jnp.moveaxis(values_all, 1, 0)))
    attended = jnp.moveaxis(per_head, 0, 1).reshape(TOKENS, HQ)
    hidden = jax.nn.gelu(jnp.dot(normed, mlp_in, preferred_element_type=jnp.float32) + mlp_bias, approximate=False).astype(jnp.bfloat16)
    head_cols = HQ // N_MP
    unit_cols = FF // N_MP

    def add_shard(shard_index, total):
        head_start = (shard_index * head_cols).astype(jnp.int32)
        unit_start = (shard_index * unit_cols).astype(jnp.int32)
        att_part = lax.dynamic_slice_in_dim(attended, head_start, head_cols, 1)
        out_part = lax.dynamic_slice_in_dim(out_weight, head_start, head_cols, 0)
        hid_part = lax.dynamic_slice_in_dim(hidden, unit_start, unit_cols, 1)
        down_part = lax.dynamic_slice_in_dim(mlp_out, unit_start, unit_cols, 0)
        term = jnp.dot(att_part, out_part, preferred_element_type=jnp.float32)
        term = term + jnp.dot(hid_part, down_part, preferred_element_type=jnp.float32)
        rounded = lax.optimization_barrier(term.astype(jnp.bfloat16))
        return total + rounded.astype(jnp.float32)
    total = lax.fori_loop(jnp.int32(0), jnp.int32(N_MP), add_shard, jnp.zeros((TOKENS, D), jnp.float32))
    return (inputs + total).astype(jnp.bfloat16)
```

```python
import functools
import math

import jax
import jax.numpy as jnp
from jax import lax
from jax.experimental import pallas as pl
from jax.experimental.pallas import tpu as pltpu
from jax.sharding import PartitionSpec as P

EPSILON = 1e-06


def normalize(values):
    centre = jnp.mean(values, axis=-1, keepdims=True)
    spread = jnp.mean(jnp.square(values - centre), axis=-1, keepdims=True)
    return (values - centre) * lax.rsqrt(spread + EPSILON)


def shards(tokens, ln_gain, qkv_weight, q_gain, k_gain, out_weight, mlp_in, mlp_bias, mlp_out):
    tok_rows = tokens.shape[0]
    gathered = lax.all_gather(tokens, "mp", axis=1, tiled=True)
    normed = (normalize(gathered.astype(jnp.float32)) * ln_gain).astype(jnp.bfloat16)
    rows_part = qkv_weight.shape[0]
    qkv_local = qkv_weight.reshape(rows_part, -1)
    pieces = (
        lax.all_gather(qkv_local, "dp", axis=0, tiled=True),
        lax.all_gather(mlp_in, "dp", axis=0, tiled=True),
    )
    projected = jnp.dot(normed, pieces[0], preferred_element_type=jnp.float32)
    pre_act = jnp.dot(normed, pieces[1], preferred_element_type=jnp.float32)
    head_count = q_gain.shape[0]
    head_size = q_gain.shape[1]
    projected = projected.reshape(tok_rows, 3, head_count, head_size)
    queries = (normalize(projected[:, 0]) * q_gain).astype(jnp.bfloat16)
    key_rows = (normalize(projected[:, 1]) * k_gain).astype(jnp.bfloat16)
    value_rows = projected[:, 2].astype(jnp.bfloat16)
    clip_keys, clip_values = (
        lax.all_gather(key_rows, "dp", axis=0, tiled=True),
        lax.all_gather(value_rows, "dp", axis=0, tiled=True),
    )
    scores = jnp.einsum("qhd,khd->hqk", queries, clip_keys, preferred_element_type=jnp.float32) * (
        1.0 / math.sqrt(head_size)
    )
    probs = jax.nn.softmax(scores, axis=-1).astype(jnp.bfloat16)
    attended = jnp.einsum("hqk,khd->qhd", probs, clip_values, preferred_element_type=jnp.float32)
    attended = attended.astype(jnp.bfloat16).reshape(tok_rows, head_count * head_size)
    hidden = jax.nn.gelu(pre_act + mlp_bias, approximate=False).astype(jnp.bfloat16)
    pieces = lax.all_gather((out_weight, mlp_out), "dp", axis=1, tiled=True)
    result = jnp.dot(attended, pieces[0], preferred_element_type=jnp.float32)
    branch_terms = result + jnp.dot(hidden, pieces[1], preferred_element_type=jnp.float32)
    summed = lax.psum_scatter(
        branch_terms.astype(jnp.bfloat16), "mp", scatter_dimension=1, tiled=True
    ).astype(jnp.float32)
    return (tokens.astype(jnp.float32) + summed).astype(jnp.bfloat16)


PLANES = 4
SLOTS = 4
BF16 = jnp.bfloat16
F32 = jnp.float32


def remote(src, dst, send, recv, device):
    return pltpu.make_async_remote_copy(
        src_ref=src, dst_ref=dst, send_sem=send, recv_sem=recv, device_id=device,
        device_id_type=pl.DeviceIdType.MESH,
    )


def fused(
    rows_at_once, chunk,
    tok, gain, wq_hbm, q_gain, k_gain, wo_hbm, wi_hbm, bias, wm_hbm, out,
    weights, total, shards_in, stage, swap, cat, from_line, from_plane, final, normed, stats, qb, kb, vb,
    w_sem, s_send, s_recv, g_send, g_recv, d_send, e_send, e_recv, a_send, a_recv, h_send, h_recv,
    y_send, y_recv, z_send, z_recv, f_send, f_recv,
):
    m = lax.axis_index("mp")
    c = lax.axis_index("dp")
    y, z = lax.rem(m, 2), m // 2
    here = z // 2
    peers = stats.shape[0]
    local, width = tok.shape
    size = rows_at_once
    half_pieces = local // size
    pieces = 2 * half_pieces
    depth = wi_hbm.shape[0]
    head_cols, units = wo_hbm.shape[0], wi_hbm.shape[1]
    own_cols, own_units = head_cols // 2, units // 2
    columns = 3 * head_cols + units
    head_size = q_gain.shape[1]
    heads = own_cols // head_size
    inner = head_cols + units
    side_line = {"mp": z * 2 + 1 - y}
    side_core = {"dp": 1 - c}
    below, above = {"mp": m - 2}, {"mp": m + 2}
    near = jnp.where(c == 0, jnp.where(z == 0, 0, 1), jnp.where(z == PLANES - 1, 1, 0))

    def lane(start, extent):
        return pl.ds(pl.multiple_of(start, 128), extent)

    def piece(p):
        return pl.ds(pl.multiple_of(p * size, size), size)

    first_weights = [
        pltpu.make_async_copy(
            wq_hbm.at[t], weights.at[pl.ds(0, depth), pl.ds(t * head_cols, head_cols)], w_sem.at[t]
        )
        for t in range(3)
    ] + [
        pltpu.make_async_copy(
            wi_hbm, weights.at[pl.ds(0, depth), pl.ds(3 * head_cols, units)], w_sem.at[3]
        )
    ]
    for copy in first_weights:
        copy.start()

    barrier = pltpu.get_barrier_semaphore()
    for k in range(1, peers):
        pl.semaphore_signal(
            barrier, inc=1, device_id={"mp": lax.rem(m + k, peers)}, device_id_type=pl.DeviceIdType.MESH
        )
    pl.semaphore_signal(barrier, inc=1, device_id=side_core, device_id_type=pl.DeviceIdType.MESH)

    values = tok[...].astype(F32)
    centre = jnp.mean(values, axis=1, keepdims=True)
    spread = jnp.sum(jnp.square(values - centre), axis=1, keepdims=True)
    even = lax.broadcasted_iota(jnp.int32, (local, 128), 1) % 2 == 0
    tile = jnp.where(even, centre, spread)
    stats[m] = jnp.transpose(tile)[0:8, :]

    pl.semaphore_wait(barrier, peers)
    for k in range(1, peers):
        other = lax.rem(m + k, peers)
        remote(stats.at[m], stats.at[m], s_send.at[k], s_recv.at[m], {"mp": other}).start()
    total[...] = jnp.zeros_like(total)
    for k in range(1, peers):
        other = lax.rem(m + k, peers)
        remote(stats.at[other], stats.at[other], s_send.at[k], s_recv.at[other], {"mp": other}).wait_recv()
    means = [stats[k, 0:1, :] for k in range(peers)]
    mean = functools.reduce(jnp.add, means) * (1.0 / peers)
    squares = functools.reduce(jnp.add, [stats[k, 1:2, :] for k in range(peers)])
    squares = squares + width * functools.reduce(jnp.add, [jnp.square(v - mean) for v in means])
    scale = lax.rsqrt(squares * (1.0 / (width * peers)) + EPSILON)
    even_row = lax.broadcasted_iota(jnp.int32, (128, local), 0) % 2 == 0
    tile = jnp.transpose(jnp.where(even_row, mean, scale))
    values = tok[...].astype(F32)
    normed[...] = ((values - tile[:, 0:1]) * tile[:, 1:2] * gain[pl.ds(m, 1), :]).astype(BF16)

    own_slot = lax.rem(m, SLOTS)

    @pl.when(c == here)
    def _():
        shards_in[own_slot, pl.ds(pl.multiple_of(c * local, local), local), :] = normed[...]

    def to_core(p):
        target = shards_in.at[own_slot, piece(c * half_pieces + p)]
        return remote(
            normed.at[piece(p)], target, d_send.at[p], g_recv.at[own_slot, c * half_pieces + p], side_core
        )

    @pl.when(c != here)
    def _():
        for p in range(half_pieces):
            to_core(p).start()

    def shard_piece(slot, p):
        return shards_in.at[slot, piece(p)]

    def gather(slot, p, way, device):
        ref = shard_piece(slot, p)
        return remote(ref, ref, g_send.at[slot, p, way], g_recv.at[slot, p], device)

    def multiply(slot, p):
        part = shards_in[slot, piece(p), :]
        depth_at = pl.ds(pl.multiple_of(slot * width, width), width)

        def column_step(j, carry):
            at = lane(j * chunk, chunk)
            total[piece(p), at] += jnp.dot(part, weights[depth_at, at], preferred_element_type=F32)
            return carry

        lax.fori_loop(0, columns // chunk, column_step, 0)

    def own_order(t):
        p = lax.rem(lax.rem(t, pieces) + c * half_pieces, pieces)
        return jnp.where(t < pieces, near, 1 - near), p

    def own_line(t, carry):
        zi, p = own_order(t)
        origin = 2 * c + zi
        slot = zi * 2 + y

        @pl.when((z != origin) | (p // half_pieces != c))
        def _():
            gather(slot, p, 2, side_line).wait_recv()

        @pl.when((z <= origin) & (z > 0))
        def _():
            gather(slot, p, 0, below).start()

        @pl.when((z >= origin) & (z < PLANES - 1))
        def _():
            gather(slot, p, 1, above).start()

        gather(slot, p, 2, side_line).start()

        @pl.when(t == 0)
        def _():
            for copy in first_weights:
                copy.wait()

        multiply(slot, p)
        return carry

    lax.fori_loop(0, 2 * pieces, own_line, 0)

    def exchange(part, p):
        return remote(
            stage.at[part, piece(p)], swap.at[part, piece(p)], e_send.at[part, p], e_recv.at[part, p], side_core
        )

    def other_line(t, carry):
        zi, p = own_order(t)
        slot = zi * 2 + 1 - y
        gather(slot, p, 2, side_line).wait_recv()
        multiply(slot, p)

        @pl.when(t >= pieces)
        def _():
            for part in range(3):
                stage[0, piece(p), pl.ds(part * own_cols, own_cols)] = total[
                    piece(p), lane(part * head_cols + (1 - c) * own_cols, own_cols)
                ].astype(BF16)
            exchange(0, p).start()
            stage[1, piece(p), pl.ds(0, own_units)] = total[
                piece(p), lane(3 * head_cols + (1 - c) * own_units, own_units)
            ].astype(BF16)
            exchange(1, p).start()

        return carry

    lax.fori_loop(0, 2 * pieces, other_line, 0)

    second_weights = [
        pltpu.make_async_copy(wo_hbm, weights.at[pl.ds(0, head_cols), pl.ds(0, depth)], w_sem.at[0]),
        pltpu.make_async_copy(wm_hbm, weights.at[pl.ds(head_cols, units), pl.ds(0, depth)], w_sem.at[1]),
    ]
    for copy in second_weights:
        copy.start()

    def heads_in(t, carry):
        _, p = own_order(t)
        exchange(0, p).wait_recv()
        for part, (target, gains) in enumerate(((qb, q_gain), (kb, k_gain), (vb, None))):
            for head in range(heads):
                at = part * own_cols + head * head_size
                block = total[
                    piece(p), lane(part * head_cols + c * own_cols + head * head_size, head_size)
                ] + swap[0, piece(p), pl.ds(at, head_size)].astype(F32)
                if gains is not None:
                    block = normalize(block) * gains[pl.ds(c * heads + head, 1), :]
                target[piece(p), pl.ds(head * head_size, head_size)] = block.astype(BF16)
        return carry

    lax.fori_loop(0, pieces, heads_in, 0)

    def attended_copy(p):
        ref = cat.at[piece(p), lane(c * own_cols, own_cols)]
        return remote(ref, ref, a_send.at[p], a_recv.at[p], side_core)

    def attended_back(p):
        ref = cat.at[piece(p), lane((1 - c) * own_cols, own_cols)]
        return remote(ref, ref, a_send.at[p], a_recv.at[p], side_core)

    def hidden_copy(p):
        ref = cat.at[piece(p), lane(head_cols + c * own_units, own_units)]
        return remote(ref, ref, h_send.at[p], h_recv.at[p], side_core)

    def hidden_back(p):
        ref = cat.at[piece(p), lane(head_cols + (1 - c) * own_units, own_units)]
        return remote(ref, ref, h_send.at[p], h_recv.at[p], side_core)

    def attend(t, carry):
        _, p = own_order(t)
        for head in range(heads):
            at = pl.ds(head * head_size, head_size)
            scores = lax.dot_general(
                qb[piece(p), at], kb[:, at], (((1,), (1,)), ((), ())), preferred_element_type=F32
            )
            top = jnp.max(scores, axis=1, keepdims=True)
            powers = jnp.exp((scores - top) * (1.0 / math.sqrt(head_size)))
            norm = jnp.sum(powers, axis=1, keepdims=True)
            result = jnp.dot(powers.astype(BF16), vb[:, at], preferred_element_type=F32) / norm
            cat[piece(p), lane(c * own_cols + head * head_size, head_size)] = result.astype(BF16)
        attended_copy(p).start()
        return carry

    lax.fori_loop(0, pieces, attend, 0)

    def activate(t, carry):
        _, p = own_order(t)
        exchange(1, p).wait_recv()
        mine = lane(3 * head_cols + c * own_units, own_units)
        before = total[piece(p), mine] + swap[1, piece(p), pl.ds(0, own_units)].astype(F32)
        before = before + bias[:, lane(c * own_units, own_units)]
        active = 0.5 * before * (1.0 + lax.erf(before * (1.0 / math.sqrt(2.0))))
        cat[piece(p), lane(head_cols + c * own_units, own_units)] = active.astype(BF16)
        hidden_copy(p).start()
        return carry

    lax.fori_loop(0, pieces, activate, 0)

    def sent(t, carry):
        zi, p = own_order(t)
        origin = 2 * c + zi
        slot = zi * 2 + y

        @pl.when((z <= origin) & (z > 0))
        def _():
            gather(slot, p, 0, below).wait_send()

        @pl.when((z >= origin) & (z < PLANES - 1))
        def _():
            gather(slot, p, 1, above).wait_send()

        gather(slot, p, 2, side_line).wait_send()

        @pl.when(t < pieces)
        def _():
            for part in range(2):
                exchange(part, p).wait_send()

        return carry

    lax.fori_loop(0, 2 * pieces, sent, 0)
    for k in range(1, peers):
        remote(stats.at[m], stats.at[m], s_send.at[k], s_recv.at[m], side_line).wait_send()

    @pl.when(c != here)
    def _():
        for p in range(half_pieces):
            to_core(p).wait_send()

    for copy in second_weights:
        copy.wait()

    def out_order(t):
        p = lax.rem(lax.rem(t, pieces) + (1 - c) * half_pieces, pieces)
        return jnp.where(t < pieces, 1 - near, near), p

    def term(p, block):
        return jnp.dot(
            cat[piece(p), :], weights[pl.ds(0, inner), lane(block * width, width)], preferred_element_type=F32
        )

    def to_line(zi, p):
        return remote(
            stage.at[zi, piece(p)], from_line.at[zi, piece(p)], y_send.at[zi, p], y_recv.at[zi, p], side_line
        )

    def other_terms(t, carry):
        zi, p = out_order(t)

        @pl.when(t < pieces)
        def _():
            attended_back(p).wait_recv()
            hidden_back(p).wait_recv()

        stage[zi, piece(p), :] = term(p, zi * 2 + 1 - y).astype(BF16)
        to_line(zi, p).start()
        return carry

    lax.fori_loop(0, 2 * pieces, other_terms, 0)

    def own_terms(t, carry):
        zi, p = out_order(t)
        total[piece(p), lane(zi * width, width)] = term(p, zi * 2 + y)
        return carry

    lax.fori_loop(0, 2 * pieces, own_terms, 0)

    def to_plane(zi, p):
        up = jnp.where(z < 2 * c + zi, 1, 0)
        return remote(
            shards_in.at[zi, piece(p)], from_plane.at[zi, 1 - up, piece(p)],
            z_send.at[zi, p], z_recv.at[zi, 1 - up, p], {"mp": m + 4 * up - 2},
        )

    def arrival(zi, side, p):
        ref = from_plane.at[zi, side, piece(p)]
        return remote(ref, ref, z_send.at[zi, p], z_recv.at[zi, side, p], side_line)

    def to_owner(zi, p):
        q = lax.rem(p, half_pieces)
        return remote(shards_in.at[zi, piece(p)], final.at[piece(q)], f_send.at[q], f_recv.at[q], side_core)

    def reduce_step(t, carry):
        zi, p = out_order(t)
        goal = 2 * c + zi
        at = lane(zi * width, width)
        to_line(zi, p).wait_recv()
        total[piece(p), at] += from_line[zi, piece(p), :].astype(F32)

        @pl.when((z <= goal) & (z > 0))
        def _():
            arrival(zi, 0, p).wait_recv()
            total[piece(p), at] += from_plane[zi, 0, piece(p), :].astype(F32)

        @pl.when((z >= goal) & (z < PLANES - 1))
        def _():
            arrival(zi, 1, p).wait_recv()
            total[piece(p), at] += from_plane[zi, 1, piece(p), :].astype(F32)

        @pl.when(z != goal)
        def _():
            shards_in[zi, piece(p), :] = total[piece(p), at].astype(BF16)
            to_plane(zi, p).start()

        @pl.when((z == goal) & (p // half_pieces != c))
        def _():
            shards_in[zi, piece(p), :] = total[piece(p), at].astype(BF16)
            to_owner(zi, p).start()

        @pl.when((z == goal) & (p // half_pieces == c))
        def _():
            q = lax.rem(p, half_pieces)
            out[piece(q), :] = (tok[piece(q), :].astype(F32) + total[piece(p), at]).astype(BF16)

        return carry

    lax.fori_loop(0, 2 * pieces, reduce_step, 0)

    @pl.when(c != here)
    def _():
        for q in range(half_pieces):
            ref = final.at[piece(q)]
            remote(ref, ref, f_send.at[q], f_recv.at[q], side_core).wait_recv()
            out[piece(q), :] = (tok[piece(q), :].astype(F32) + final[piece(q), :].astype(F32)).astype(BF16)

    def finish(t, carry):
        zi, p = out_order(t)
        to_line(zi, p).wait_send()

        @pl.when(z != 2 * c + zi)
        def _():
            to_plane(zi, p).wait_send()

        @pl.when((z == 2 * c + zi) & (p // half_pieces != c))
        def _():
            to_owner(zi, p).wait_send()

        @pl.when(t < pieces)
        def _():
            attended_copy(p).wait_send()
            hidden_copy(p).wait_send()

        return carry

    lax.fori_loop(0, 2 * pieces, finish, 0)


def fused_shards(tokens, ln_gain, qkv_weight, q_gain, k_gain, out_weight, mlp_in, mlp_bias, mlp_out):
    local, width = tokens.shape
    depth, _, head_cols = qkv_weight.shape
    units = mlp_in.shape[1]
    half = out_weight.shape[1]
    peers = ln_gain.shape[0] // width
    rows = 2 * local
    size = local // HALF_PIECES
    pieces = 2 * HALF_PIECES
    columns = 3 * head_cols + units
    inner = head_cols + units
    chunk = 512
    vmem, hbm = pl.BlockSpec(memory_space=pltpu.VMEM), pl.BlockSpec(memory_space=pl.ANY)
    dma = pltpu.SemaphoreType.DMA
    return pl.pallas_call(
        functools.partial(fused, size, chunk),
        out_shape=jax.ShapeDtypeStruct(tokens.shape, BF16),
        in_specs=[vmem, vmem, hbm, vmem, vmem, hbm, hbm, vmem, hbm],
        out_specs=vmem,
        scratch_shapes=[
            pltpu.VMEM((max(depth, inner), max(columns, half)), BF16),
            pltpu.VMEM((rows, columns), F32),
            pltpu.VMEM((SLOTS, rows, width), BF16),
            pltpu.VMEM((2, rows, width), BF16),
            pltpu.VMEM((2, rows, width), BF16),
            pltpu.VMEM((rows, inner), BF16),
            pltpu.VMEM((2, rows, width), BF16),
            pltpu.VMEM((2, 2, rows, width), BF16),
            pltpu.VMEM((local, width), BF16),
            pltpu.VMEM((local, width), BF16),
            pltpu.VMEM((peers, 8, local), F32),
            pltpu.VMEM((rows, head_cols // 2), BF16),
            pltpu.VMEM((rows, head_cols // 2), BF16),
            pltpu.VMEM((rows, head_cols // 2), BF16),
            dma((4,)), dma((peers,)), dma((peers,)), dma((SLOTS, pieces, 3)), dma((SLOTS, pieces)),
            dma((HALF_PIECES,)), dma((2, pieces)), dma((2, pieces)),
            dma((pieces,)), dma((pieces,)), dma((pieces,)), dma((pieces,)),
            dma((2, pieces)), dma((2, pieces)), dma((2, pieces)), dma((2, 2, pieces)),
            dma((HALF_PIECES,)), dma((HALF_PIECES,)),
        ],
        compiler_params=pltpu.CompilerParams(
            collective_id=0, has_side_effects=True, vmem_limit_bytes=VMEM_BYTES
        ),
    )(
        tokens, ln_gain.reshape(peers, width), jnp.transpose(qkv_weight, (1, 0, 2)), q_gain, k_gain,
        out_weight, mlp_in, mlp_bias.reshape(1, units), mlp_out,
    )


HALF_PIECES = 2
VMEM_BYTES = 63 * 1024 * 1024


def fits(mesh, tokens, ln_gain, qkv_weight, q_gain, k_gain, out_weight, mlp_in, mlp_bias, mlp_out):
    peers, cores = mesh.shape["mp"], mesh.shape["dp"]
    if peers != 2 * PLANES or cores != 2:
        return False
    local = tokens.shape[0] // (mesh.shape["pool"] * cores)
    width = tokens.shape[1] // peers
    head_cols = out_weight.shape[0] // peers
    units = mlp_in.shape[1] // peers
    columns = 3 * head_cols + units
    return (
        local % (16 * HALF_PIECES) == 0 and local % 128 == 0 and width % 128 == 0
        and q_gain.shape[1] == 128 and head_cols % 256 == 0 and units % 256 == 0 and columns % 512 == 0
        and max(3 * head_cols // 2, units // 2) <= width and 2 * width <= columns
        and local * peers * width <= 512 * 6144 and head_cols <= 512 and units <= 1536
    )


def solution(mesh):
    def run(*args):
        body = fused_shards if fits(mesh, *args) else shards
        return mapped(mesh, body)(*args)

    return run


def mapped(mesh, body):
    return jax.shard_map(
        body,
        mesh=mesh,
        in_specs=(
            P(("pool", "dp"), "mp"),
            P(),
            P("dp", None, "mp"),
            P("mp", None),
            P("mp", None),
            P("mp", "dp"),
            P("dp", "mp"),
            P("mp"),
            P("mp", "dp"),
        ),
        out_specs=P(("pool", "dp"), "mp"),
        check_vma=False,
    )
```

```python
import functools
import math

import jax
import jax.numpy as jnp
from jax import lax
from jax.experimental import pallas as pl
from jax.experimental.pallas import tpu as pltpu
from jax.sharding import PartitionSpec as P

EPSILON = 1e-06


def normalize(values):
    centre = jnp.mean(values, axis=-1, keepdims=True)
    spread = jnp.mean(jnp.square(values - centre), axis=-1, keepdims=True)
    return (values - centre) * lax.rsqrt(spread + EPSILON)


def shards(tokens, ln_gain, qkv_weight, q_gain, k_gain, out_weight, mlp_in, mlp_bias, mlp_out):
    tok_rows = tokens.shape[0]
    gathered = lax.all_gather(tokens, "mp", axis=1, tiled=True)
    normed = (normalize(gathered.astype(jnp.float32)) * ln_gain).astype(jnp.bfloat16)
    rows_part = qkv_weight.shape[0]
    qkv_local = qkv_weight.reshape(rows_part, -1)
    pieces = (
        lax.all_gather(qkv_local, "dp", axis=0, tiled=True),
        lax.all_gather(mlp_in, "dp", axis=0, tiled=True),
    )
    projected = jnp.dot(normed, pieces[0], preferred_element_type=jnp.float32)
    pre_act = jnp.dot(normed, pieces[1], preferred_element_type=jnp.float32)
    head_count = q_gain.shape[0]
    head_size = q_gain.shape[1]
    projected = projected.reshape(tok_rows, 3, head_count, head_size)
    queries = (normalize(projected[:, 0]) * q_gain).astype(jnp.bfloat16)
    key_rows = (normalize(projected[:, 1]) * k_gain).astype(jnp.bfloat16)
    value_rows = projected[:, 2].astype(jnp.bfloat16)
    clip_keys, clip_values = (
        lax.all_gather(key_rows, "dp", axis=0, tiled=True),
        lax.all_gather(value_rows, "dp", axis=0, tiled=True),
    )
    scores = jnp.einsum("qhd,khd->hqk", queries, clip_keys, preferred_element_type=jnp.float32) * (
        1.0 / math.sqrt(head_size)
    )
    probs = jax.nn.softmax(scores, axis=-1).astype(jnp.bfloat16)
    attended = jnp.einsum("hqk,khd->qhd", probs, clip_values, preferred_element_type=jnp.float32)
    attended = attended.astype(jnp.bfloat16).reshape(tok_rows, head_count * head_size)
    hidden = jax.nn.gelu(pre_act + mlp_bias, approximate=False).astype(jnp.bfloat16)
    pieces = lax.all_gather((out_weight, mlp_out), "dp", axis=1, tiled=True)
    result = jnp.dot(attended, pieces[0], preferred_element_type=jnp.float32)
    branch_terms = result + jnp.dot(hidden, pieces[1], preferred_element_type=jnp.float32)
    summed = lax.psum_scatter(
        branch_terms.astype(jnp.bfloat16), "mp", scatter_dimension=1, tiled=True
    ).astype(jnp.float32)
    return (tokens.astype(jnp.float32) + summed).astype(jnp.bfloat16)


PLANES = 4
SLOTS = 4
BF16 = jnp.bfloat16
F32 = jnp.float32


def remote(src, dst, send, recv, device):
    return pltpu.make_async_remote_copy(
        src_ref=src, dst_ref=dst, send_sem=send, recv_sem=recv, device_id=device,
        device_id_type=pl.DeviceIdType.MESH,
    )


def fused(
    rows_at_once, chunk,
    tok, gain, wq_hbm, q_gain, k_gain, wo_hbm, wi_hbm, bias, wm_hbm, out,
    weights, total, shards_in, stage, swap, cat, from_line, from_plane, from_chain, normed, stats, qb, kb, vb,
    w_sem, s_send, s_recv, g_send, g_recv, d_send, e_send, e_recv, a_send, a_recv, h_send, h_recv,
    y_send, y_recv, z_send, z_recv, c_recv, f_send, f_recv,
):
    m = lax.axis_index("mp")
    c = lax.axis_index("dp")
    y, z = lax.rem(m, 2), m // 2
    here = z // 2
    peers = stats.shape[0]
    local, width = tok.shape
    size = rows_at_once
    half_pieces = local // size
    pieces = 2 * half_pieces
    depth = wi_hbm.shape[0]
    head_cols, units = wo_hbm.shape[0], wi_hbm.shape[1]
    own_cols, own_units = head_cols // 2, units // 2
    columns = 3 * head_cols + units
    head_size = q_gain.shape[1]
    heads = own_cols // head_size
    inner = head_cols + units
    side_line = {"mp": z * 2 + 1 - y}
    side_core = {"dp": 1 - c}
    below, above = {"mp": m - 2}, {"mp": m + 2}
    near = jnp.where(c == 0, jnp.where(z == 0, 0, 1), jnp.where(z == PLANES - 1, 1, 0))
    outer = (PLANES - 1) * c

    def crosses_once(zi, p):
        return (zi == c) & (p < half_pieces)

    def crosses_here(zi, p):
        return (zi != c) | (p >= half_pieces) | (z == outer)

    def lane(start, extent):
        return pl.ds(pl.multiple_of(start, 128), extent)

    def piece(p):
        return pl.ds(pl.multiple_of(p * size, size), size)

    first_weights = [
        pltpu.make_async_copy(
            wq_hbm.at[t], weights.at[pl.ds(0, depth), pl.ds(t * head_cols, head_cols)], w_sem.at[t]
        )
        for t in range(3)
    ] + [
        pltpu.make_async_copy(
            wi_hbm, weights.at[pl.ds(0, depth), pl.ds(3 * head_cols, units)], w_sem.at[3]
        )
    ]
    for copy in first_weights:
        copy.start()

    barrier = pltpu.get_barrier_semaphore()
    for k in range(1, peers):
        pl.semaphore_signal(
            barrier, inc=1, device_id={"mp": lax.rem(m + k, peers)}, device_id_type=pl.DeviceIdType.MESH
        )
    pl.semaphore_signal(barrier, inc=1, device_id=side_core, device_id_type=pl.DeviceIdType.MESH)

    values = tok[...].astype(F32)
    centre = jnp.mean(values, axis=1, keepdims=True)
    spread = jnp.sum(jnp.square(values - centre), axis=1, keepdims=True)
    even = lax.broadcasted_iota(jnp.int32, (local, 128), 1) % 2 == 0
    tile = jnp.where(even, centre, spread)
    stats[m] = jnp.transpose(tile)[0:8, :]

    pl.semaphore_wait(barrier, peers)
    for k in range(1, peers):
        other = lax.rem(m + k, peers)
        remote(stats.at[m], stats.at[m], s_send.at[k], s_recv.at[m], {"mp": other}).start()
    total[...] = jnp.zeros_like(total)
    for k in range(1, peers):
        other = lax.rem(m + k, peers)
        remote(stats.at[other], stats.at[other], s_send.at[k], s_recv.at[other], {"mp": other}).wait_recv()
    means = [stats[k, 0:1, :] for k in range(peers)]
    mean = functools.reduce(jnp.add, means) * (1.0 / peers)
    squares = functools.reduce(jnp.add, [stats[k, 1:2, :] for k in range(peers)])
    squares = squares + width * functools.reduce(jnp.add, [jnp.square(v - mean) for v in means])
    scale = lax.rsqrt(squares * (1.0 / (width * peers)) + EPSILON)
    even_row = lax.broadcasted_iota(jnp.int32, (128, local), 0) % 2 == 0
    tile = jnp.transpose(jnp.where(even_row, mean, scale))
    values = tok[...].astype(F32)
    normed[...] = ((values - tile[:, 0:1]) * tile[:, 1:2] * gain[pl.ds(m, 1), :]).astype(BF16)

    own_slot = lax.rem(m, SLOTS)

    @pl.when(c == here)
    def _():
        shards_in[own_slot, pl.ds(pl.multiple_of(c * local, local), local), :] = normed[...]

    def to_core(p):
        target = shards_in.at[own_slot, piece(c * half_pieces + p)]
        return remote(
            normed.at[piece(p)], target, d_send.at[p], g_recv.at[own_slot, c * half_pieces + p], side_core
        )

    @pl.when(c != here)
    def _():
        for p in range(half_pieces):
            to_core(p).start()

    def shard_piece(slot, p):
        return shards_in.at[slot, piece(p)]

    def gather(slot, p, way, device):
        ref = shard_piece(slot, p)
        return remote(ref, ref, g_send.at[slot, p, way], g_recv.at[slot, p], device)

    def multiply(slot, p):
        part = shards_in[slot, piece(p), :]
        depth_at = pl.ds(pl.multiple_of(slot * width, width), width)

        def column_step(j, carry):
            at = lane(j * chunk, chunk)
            total[piece(p), at] += jnp.dot(part, weights[depth_at, at], preferred_element_type=F32)
            return carry

        lax.fori_loop(0, columns // chunk, column_step, 0)

    def own_order(t):
        return jnp.where(t < pieces, near, 1 - near), lax.rem(t, pieces)

    def own_line(t, carry):
        zi, p = own_order(t)
        origin = 2 * c + zi
        slot = zi * 2 + y

        @pl.when((z != origin) | (p // half_pieces != c))
        def _():
            gather(slot, p, 2, side_line).wait_recv()

        @pl.when((z <= origin) & (z > 0))
        def _():
            gather(slot, p, 0, below).start()

        @pl.when((z >= origin) & (z < PLANES - 1))
        def _():
            gather(slot, p, 1, above).start()

        @pl.when(crosses_here(zi, p))
        def _():
            gather(slot, p, 2, side_line).start()

        @pl.when(t == 0)
        def _():
            for copy in first_weights:
                copy.wait()

        multiply(slot, p)

        @pl.when(t >= pieces + half_pieces)
        def _():
            other = c * 2 + 1 - y
            q = p - half_pieces
            gather(other, q, 2, side_line).wait_recv()
            pass_on(other, q, lambda copy: copy.start())
            multiply(other, q)

        return carry

    def pass_on(slot, p, act):
        @pl.when((c == 0) & (z < PLANES - 1))
        def _():
            act(gather(slot, p, 1, above))

        @pl.when((c == 1) & (z > 0))
        def _():
            act(gather(slot, p, 0, below))

    lax.fori_loop(0, 2 * pieces, own_line, 0)

    def exchange(part, p):
        return remote(
            stage.at[part, piece(p)], swap.at[part, piece(p)], e_send.at[part, p], e_recv.at[part, p], side_core
        )

    def other_line(t, carry):
        zi, p = own_order(t)
        slot = zi * 2 + 1 - y

        @pl.when(jnp.logical_not(crosses_once(zi, p)))
        def _():
            gather(slot, p, 2, side_line).wait_recv()
            multiply(slot, p)

        @pl.when(t >= pieces)
        def _():
            for part in range(3):
                stage[0, piece(p), pl.ds(part * own_cols, own_cols)] = total[
                    piece(p), lane(part * head_cols + (1 - c) * own_cols, own_cols)
                ].astype(BF16)
            exchange(0, p).start()
            stage[1, piece(p), pl.ds(0, own_units)] = total[
                piece(p), lane(3 * head_cols + (1 - c) * own_units, own_units)
            ].astype(BF16)
            exchange(1, p).start()

        @pl.when(t > pieces)
        def _():
            finish_rows(p - 1)

        return carry

    def heads_in(p):
        exchange(0, p).wait_recv()
        for part, (target, gains) in enumerate(((qb, q_gain), (kb, k_gain), (vb, None))):
            for head in range(heads):
                at = part * own_cols + head * head_size
                block = total[
                    piece(p), lane(part * head_cols + c * own_cols + head * head_size, head_size)
                ] + swap[0, piece(p), pl.ds(at, head_size)].astype(F32)
                if gains is not None:
                    block = normalize(block) * gains[pl.ds(c * heads + head, 1), :]
                target[piece(p), pl.ds(head * head_size, head_size)] = block.astype(BF16)

    def attended_copy(p):
        ref = cat.at[piece(p), lane(c * own_cols, own_cols)]
        return remote(ref, ref, a_send.at[p], a_recv.at[p], side_core)

    def attended_back(p):
        ref = cat.at[piece(p), lane((1 - c) * own_cols, own_cols)]
        return remote(ref, ref, a_send.at[p], a_recv.at[p], side_core)

    def hidden_copy(p):
        ref = cat.at[piece(p), lane(head_cols + c * own_units, own_units)]
        return remote(ref, ref, h_send.at[p], h_recv.at[p], side_core)

    def hidden_back(p):
        ref = cat.at[piece(p), lane(head_cols + (1 - c) * own_units, own_units)]
        return remote(ref, ref, h_send.at[p], h_recv.at[p], side_core)

    def attend(p):
        for head in range(heads):
            at = pl.ds(head * head_size, head_size)
            scores = lax.dot_general(
                qb[piece(p), at], kb[:, at], (((1,), (1,)), ((), ())), preferred_element_type=F32
            )
            top = jnp.max(scores, axis=1, keepdims=True)
            powers = jnp.exp((scores - top) * (1.0 / math.sqrt(head_size)))
            norm = jnp.sum(powers, axis=1, keepdims=True)
            result = jnp.dot(powers.astype(BF16), vb[:, at], preferred_element_type=F32) / norm
            cat[piece(p), lane(c * own_cols + head * head_size, head_size)] = result.astype(BF16)
        attended_copy(p).start()

    def activate(p):
        exchange(1, p).wait_recv()
        mine = lane(3 * head_cols + c * own_units, own_units)
        before = total[piece(p), mine] + swap[1, piece(p), pl.ds(0, own_units)].astype(F32)
        before = before + bias[:, lane(c * own_units, own_units)]
        active = 0.5 * before * (1.0 + lax.erf(before * (1.0 / math.sqrt(2.0))))
        cat[piece(p), lane(head_cols + c * own_units, own_units)] = active.astype(BF16)
        hidden_copy(p).start()

    def finish_rows(p):
        heads_in(p)
        activate(p)

    lax.fori_loop(0, 2 * pieces, other_line, 0)

    second_weights = [
        pltpu.make_async_copy(wo_hbm, weights.at[pl.ds(0, head_cols), pl.ds(0, depth)], w_sem.at[0]),
        pltpu.make_async_copy(wm_hbm, weights.at[pl.ds(head_cols, units), pl.ds(0, depth)], w_sem.at[1]),
    ]
    for copy in second_weights:
        copy.start()

    finish_rows(pieces - 1)

    def sent(t, carry):
        zi, p = own_order(t)
        origin = 2 * c + zi
        slot = zi * 2 + y

        @pl.when((z <= origin) & (z > 0))
        def _():
            gather(slot, p, 0, below).wait_send()

        @pl.when((z >= origin) & (z < PLANES - 1))
        def _():
            gather(slot, p, 1, above).wait_send()

        @pl.when(crosses_here(zi, p))
        def _():
            gather(slot, p, 2, side_line).wait_send()

        @pl.when(t < half_pieces)
        def _():
            pass_on(c * 2 + 1 - y, p, lambda copy: copy.wait_send())

        @pl.when(t < pieces)
        def _():
            for part in range(2):
                exchange(part, p).wait_send()

        return carry

    lax.fori_loop(0, 2 * pieces, sent, 0)
    for k in range(1, peers):
        remote(stats.at[m], stats.at[m], s_send.at[k], s_recv.at[m], side_line).wait_send()

    @pl.when(c != here)
    def _():
        for p in range(half_pieces):
            to_core(p).wait_send()

    for copy in second_weights:
        copy.wait()

    def out_order(t):
        p = lax.rem(lax.rem(t, pieces) + half_pieces, pieces)
        return jnp.where(t < pieces, 1 - near, near), p

    def term(p, block):
        return jnp.dot(
            cat[piece(p), :], weights[pl.ds(0, inner), lane(block * width, width)], preferred_element_type=F32
        )

    def to_line(zi, p):
        return remote(
            stage.at[zi, piece(p)], from_line.at[zi, piece(p)], y_send.at[zi, p], y_recv.at[zi, p], side_line
        )

    def other_terms(t):
        zi, p = out_order(t)

        @pl.when(t < pieces)
        def _():
            attended_back(p).wait_recv()
            hidden_back(p).wait_recv()

        value = term(p, zi * 2 + 1 - y)

        @pl.when(jnp.logical_not(crosses_once(zi, p)))
        def _():
            stage[zi, piece(p), :] = value.astype(BF16)
            to_line(zi, p).start()

        @pl.when(crosses_once(zi, p) & (z == PLANES - 1 - outer))
        def _():
            stage[zi, piece(p), :] = value.astype(BF16)

        @pl.when(crosses_once(zi, p) & (z != PLANES - 1 - outer))
        def _():
            q = lax.rem(p, half_pieces)
            along(zi, q).wait_recv()
            stage[zi, piece(p), :] = (value + from_chain[piece(q), :].astype(F32)).astype(BF16)

        @pl.when(crosses_once(zi, p) & (z == outer))
        def _():
            to_line(zi, p).start()

        @pl.when(crosses_once(zi, p) & (z != outer))
        def _():
            along(zi, lax.rem(p, half_pieces)).start()

    def along(zi, q):
        return remote(
            stage.at[zi, piece(q)], from_chain.at[piece(q)], y_send.at[zi, q], c_recv.at[q], {"mp": m + 4 * c - 2}
        )

    def attend_and_terms(t, carry):
        @pl.when(t < pieces)
        def _():
            attend(out_order(t)[1])

        @pl.when(t > 0)
        def _():
            other_terms(t - 1)

        return carry

    lax.fori_loop(0, 2 * pieces + 1, attend_and_terms, 0)

    def own_terms(t, carry):
        zi, p = out_order(t)
        total[piece(p), lane(zi * width, width)] = term(p, zi * 2 + y)
        return carry

    lax.fori_loop(0, 2 * pieces, own_terms, 0)

    def to_plane(zi, p):
        up = jnp.where(z < 2 * c + zi, 1, 0)
        return remote(
            shards_in.at[zi, piece(p)], from_plane.at[zi, 1 - up, piece(p)],
            z_send.at[zi, p], z_recv.at[zi, 1 - up, p], {"mp": m + 4 * up - 2},
        )

    def arrival(zi, side, p):
        ref = from_plane.at[zi, side, piece(p)]
        return remote(ref, ref, z_send.at[zi, p], z_recv.at[zi, side, p], side_line)

    def to_owner(zi, p):
        q = lax.rem(p, half_pieces)
        return remote(shards_in.at[zi, piece(p)], normed.at[piece(q)], f_send.at[q], f_recv.at[q], side_core)

    def reduce_step(t, carry):
        zi, p = out_order(t)
        goal = 2 * c + zi
        at = lane(zi * width, width)

        @pl.when(crosses_here(zi, p))
        def _():
            to_line(zi, p).wait_recv()
            total[piece(p), at] += from_line[zi, piece(p), :].astype(F32)

        @pl.when((z <= goal) & (z > 0))
        def _():
            arrival(zi, 0, p).wait_recv()
            total[piece(p), at] += from_plane[zi, 0, piece(p), :].astype(F32)

        @pl.when((z >= goal) & (z < PLANES - 1))
        def _():
            arrival(zi, 1, p).wait_recv()
            total[piece(p), at] += from_plane[zi, 1, piece(p), :].astype(F32)

        @pl.when(z != goal)
        def _():
            shards_in[zi, piece(p), :] = total[piece(p), at].astype(BF16)
            to_plane(zi, p).start()

        @pl.when((z == goal) & (p // half_pieces != c))
        def _():
            shards_in[zi, piece(p), :] = total[piece(p), at].astype(BF16)
            to_owner(zi, p).start()

        @pl.when((z == goal) & (p // half_pieces == c))
        def _():
            q = lax.rem(p, half_pieces)
            out[piece(q), :] = (tok[piece(q), :].astype(F32) + total[piece(p), at]).astype(BF16)

        return carry

    lax.fori_loop(0, 2 * pieces, reduce_step, 0)

    @pl.when(c != here)
    def _():
        for q in range(half_pieces):
            ref = normed.at[piece(q)]
            remote(ref, ref, f_send.at[q], f_recv.at[q], side_core).wait_recv()
            out[piece(q), :] = (tok[piece(q), :].astype(F32) + normed[piece(q), :].astype(F32)).astype(BF16)

    def finish(t, carry):
        zi, p = out_order(t)
        to_line(zi, p).wait_send()

        @pl.when(z != 2 * c + zi)
        def _():
            to_plane(zi, p).wait_send()

        @pl.when((z == 2 * c + zi) & (p // half_pieces != c))
        def _():
            to_owner(zi, p).wait_send()

        @pl.when(t < pieces)
        def _():
            attended_copy(p).wait_send()
            hidden_copy(p).wait_send()

        return carry

    lax.fori_loop(0, 2 * pieces, finish, 0)


def fused_shards(tokens, ln_gain, qkv_weight, q_gain, k_gain, out_weight, mlp_in, mlp_bias, mlp_out):
    local, width = tokens.shape
    depth, _, head_cols = qkv_weight.shape
    units = mlp_in.shape[1]
    half = out_weight.shape[1]
    peers = ln_gain.shape[0] // width
    rows = 2 * local
    size = local // HALF_PIECES
    pieces = 2 * HALF_PIECES
    columns = 3 * head_cols + units
    inner = head_cols + units
    chunk = 512
    vmem, hbm = pl.BlockSpec(memory_space=pltpu.VMEM), pl.BlockSpec(memory_space=pl.ANY)
    dma = pltpu.SemaphoreType.DMA
    return pl.pallas_call(
        functools.partial(fused, size, chunk),
        out_shape=jax.ShapeDtypeStruct(tokens.shape, BF16),
        in_specs=[vmem, vmem, hbm, vmem, vmem, hbm, hbm, vmem, hbm],
        out_specs=vmem,
        scratch_shapes=[
            pltpu.VMEM((max(depth, inner), max(columns, half)), BF16),
            pltpu.VMEM((rows, columns), F32),
            pltpu.VMEM((SLOTS, rows, width), BF16),
            pltpu.VMEM((2, rows, width), BF16),
            pltpu.VMEM((2, rows, width), BF16),
            pltpu.VMEM((rows, inner), BF16),
            pltpu.VMEM((2, rows, width), BF16),
            pltpu.VMEM((2, 2, rows, width), BF16),
            pltpu.VMEM((local, width), BF16),
            pltpu.VMEM((local, width), BF16),
            pltpu.VMEM((peers, 8, local), F32),
            pltpu.VMEM((rows, head_cols // 2), BF16),
            pltpu.VMEM((rows, head_cols // 2), BF16),
            pltpu.VMEM((rows, head_cols // 2), BF16),
            dma((4,)), dma((peers,)), dma((peers,)), dma((SLOTS, pieces, 3)), dma((SLOTS, pieces)),
            dma((HALF_PIECES,)), dma((2, pieces)), dma((2, pieces)),
            dma((pieces,)), dma((pieces,)), dma((pieces,)), dma((pieces,)),
            dma((2, pieces)), dma((2, pieces)), dma((2, pieces)), dma((2, 2, pieces)), dma((HALF_PIECES,)),
            dma((HALF_PIECES,)), dma((HALF_PIECES,)),
        ],
        compiler_params=pltpu.CompilerParams(
            collective_id=0, has_side_effects=True, vmem_limit_bytes=VMEM_BYTES
        ),
    )(
        tokens, ln_gain.reshape(peers, width), jnp.transpose(qkv_weight, (1, 0, 2)), q_gain, k_gain,
        out_weight, mlp_in, mlp_bias.reshape(1, units), mlp_out,
    )


HALF_PIECES = 2
VMEM_BYTES = 63 * 1024 * 1024


def fits(mesh, tokens, ln_gain, qkv_weight, q_gain, k_gain, out_weight, mlp_in, mlp_bias, mlp_out):
    peers, cores = mesh.shape["mp"], mesh.shape["dp"]
    if peers != 2 * PLANES or cores != 2:
        return False
    local = tokens.shape[0] // (mesh.shape["pool"] * cores)
    width = tokens.shape[1] // peers
    head_cols = out_weight.shape[0] // peers
    units = mlp_in.shape[1] // peers
    columns = 3 * head_cols + units
    return (
        local % (16 * HALF_PIECES) == 0 and local % 128 == 0 and width % 128 == 0
        and q_gain.shape[1] == 128 and head_cols % 256 == 0 and units % 256 == 0 and columns % 512 == 0
        and max(3 * head_cols // 2, units // 2) <= width and 2 * width <= columns
        and local * peers * width <= 512 * 6144 and head_cols <= 512 and units <= 1536
    )


def solution(mesh):
    def run(*args):
        body = fused_shards if fits(mesh, *args) else shards
        return mapped(mesh, body)(*args)

    return run


def mapped(mesh, body):
    return jax.shard_map(
        body,
        mesh=mesh,
        in_specs=(
            P(("pool", "dp"), "mp"),
            P(),
            P("dp", None, "mp"),
            P("mp", None),
            P("mp", None),
            P("mp", "dp"),
            P("dp", "mp"),
            P("mp"),
            P("mp", "dp"),
        ),
        out_specs=P(("pool", "dp"), "mp"),
        check_vma=False,
    )
```
